32 devices in a mesh: gx: 8 (over y, x, core), gy: 4 (over z).
Axes of the slice: x: 2, y: 2, z: 4, core: 2. Of those that a mesh axis runs over, the one named last changes fastest.
Arguments:
- features: bfloat16 [8, 4, 8, 128, 128], P('gx', 'gy'), may hold values from -6 to 6
- positions: float32 [8, 4, 8, 3, 128], P('gx', 'gy'), may hold values from 0 to 1
- species: int32 [8, 4, 8, 128], P('gx', 'gy'), may hold values from 0 to 7
- atom_mask: int32 [8, 4, 8, 128], P('gx', 'gy'), may hold values 0 or 1
- charge_table: float32 [8, 64], replicated, may hold values from -5 to 5
- k_vectors: float32 [3, 512], replicated, may hold values from -1.5 to 1.5
- k_weights: float32 [512], replicated, may hold values from 0.2 to 2
- w_value: bfloat16 [2, 128, 64], replicated, may hold values from -0.5 to 0.5
- w_charge: bfloat16 [2, 128, 64], replicated, may hold values from -0.5 to 0.5
- w_radial: float32 [2, 8, 64], replicated, may hold values from -1.8 to 1.8
- w_out: bfloat16 [2, 64, 128], replicated, may hold values from -0.75 to 0.75
Outputs:
- features_out: bfloat16 [8, 4, 8, 128, 128], P('gx', 'gy')
- potential: float32 [8, 4, 8, 64, 128], P('gx', 'gy')
The draws below stay inside these ranges and needn't reach their ends.
All inputs are finite; a program needn't handle non-finite values. No bound on the sum of `atom_mask` on one device may be relied on, other than what follows from the above.
Results may differ from the reference program's by a relative error of at most 0.005.
Values may be sent and summed in bfloat16 or wider, within the bound.
A program may use at most 64 MiB of HBM per device.

```python
import math
import jax
import jax.numpy as jnp
from jax import lax

D = 128
C = 64
K = 512
M = 8
NSPEC = 8
A = 128
LAYERS = 2
ZBLOCK = 4
CZ = 8
NCX = 8
NCY = 4


def set_ends(values, rng, least, high):
    longest = values.shape.index(max(values.shape))
    spots = []
    for shift in (0, 1):
        where = [jax.random.randint(jax.random.fold_in(rng, axis), (), 0, length) for axis, length in enumerate(values.shape)]
        where[longest] = (where[longest] + shift) % values.shape[longest]
        spots.append(tuple(where))
    return values.at[spots[0]].set(least).at[spots[1]].set(high)


def block_scale(own_key, dims, pieces, least, high):
    def one(position, shards_of):
        heights = jax.random.uniform(jax.random.fold_in(jax.random.fold_in(own_key, 6), position), (shards_of,), jnp.float32, least / len(pieces), high / len(pieces))
        return jnp.repeat(jnp.exp(heights), dims[position] // shards_of).reshape((-1,) + (1,) * (len(dims) - position - 1))

    level = one(*pieces[0])
    for cut in pieces[1:]:
        level = level * one(*cut)
    return level


def scatter_about(rng, shape, deviation, reach, shards=(), held_as=jnp.bfloat16):
    values = jax.random.normal(rng, shape, jnp.float32) * deviation
    if len(shards) > 0:
        values = block_scale(rng, shape, shards, -0.22, 0.18) * values
    return jnp.clip(values, min=-reach, max=reach).astype(held_as)


def setup_inputs(seed: int = 0) -> dict:
    splits = jax.random.split(jax.random.key(seed), 12)
    features = scatter_about(splits[0], (NCX, NCY, CZ, D, A), 1.0, 6.0, ((0, 8), (1, 4)))
    positions = jnp.clip(1.0 * jax.random.uniform(splits[1], (NCX, NCY, CZ, 3, A), jnp.float32) ** block_scale(splits[1], (NCX, NCY, CZ, 3, A), ((0, 8), (1, 4)), -0.2, 0.2), 0.0, 1.0)
    species = set_ends(jax.random.randint(splits[2], (NCX, NCY, CZ, A), 0, NSPEC), jax.random.fold_in(splits[2], 1), 0, NSPEC - 1).astype(jnp.int32)
    atom_mask = set_ends((jax.random.randint(splits[3], (NCX, NCY, CZ, A), 0, 4) < 3).astype(jnp.int32), jax.random.fold_in(splits[3], 1), 0, 1)
    charge_table = scatter_about(splits[4], (NSPEC, C), 1.0, 5.0, (), jnp.float32)
    k_vectors = jnp.clip(jax.random.uniform(splits[5], (3, K), jnp.float32, -1.5, 1.5), -1.5, 1.5)
    k_weights = jnp.clip(jnp.exp(jax.random.uniform(splits[6], (K,), jnp.float32, math.log(0.2), math.log(2.0))), 0.2, 2.0)
    w_value = scatter_about(splits[7], (LAYERS, D, C), D ** -0.5, 0.5)
    w_charge = scatter_about(splits[8], (LAYERS, D, C), D ** -0.5, 0.5)
    w_radial = scatter_about(splits[9], (LAYERS, M, C), 0.3, 1.8, (), jnp.float32)
    w_out = scatter_about(splits[10], (LAYERS, C, D), C ** -0.5, 0.75)
    return {"features": features, "positions": positions, "species": species, "atom_mask": atom_mask, "charge_table": charge_table, "k_vectors": k_vectors, "k_weights": k_weights, "w_value": w_value, "w_charge": w_charge, "w_radial": w_radial, "w_out": w_out}


def cell_messages(ext_pos, ext_val, radial_mix, z_index):
    atom_count = ext_pos.shape[-1]
    chan_count = ext_val.shape[-2]
    basis_count = radial_mix.shape[0]
    near_pos = lax.dynamic_slice_in_dim(ext_pos, z_index, 3, 2)
    shifts = jnp.arange(3, dtype=jnp.float32) - 1.0
    grid_shift = jnp.stack(jnp.meshgrid(shifts, shifts, shifts, indexing='ij'), axis=-1)
    near_pos = near_pos + grid_shift[..., None]
    near_pos = jnp.moveaxis(near_pos, 3, 0).reshape(3, 27 * atom_count)
    centre = lax.dynamic_index_in_dim(ext_pos[1, 1], z_index + 1, 0, keepdims=False)
    offset_vec = near_pos[:, None, :] - centre[:, :, None]
    dist_sq = lax.optimization_barrier(jnp.sum(offset_vec * offset_vec, axis=0))
    row_ids = lax.broadcasted_iota(jnp.int32, dist_sq.shape, 0)
    col_ids = lax.broadcasted_iota(jnp.int32, dist_sq.shape, 1)
    keep = (dist_sq < 1.0) & (col_ids != row_ids + 13 * atom_count)
    envelope = jnp.where(keep, jnp.square(1.0 - dist_sq), 0.0)
    radius = jnp.sqrt(dist_sq)
    centres = (jnp.arange(basis_count, dtype=jnp.float32) + 0.5) / basis_count
    basis_vals = (jnp.exp(-jnp.square((radius[None] - centres[:, None, None]) * basis_count)) * envelope[None]).astype(jnp.bfloat16)
    near_val = lax.dynamic_slice_in_dim(ext_val, z_index, 3, 2)
    near_val = jnp.moveaxis(near_val.reshape(27, chan_count, atom_count), 1, 0).reshape(chan_count, 27 * atom_count)
    partial_value = jnp.einsum('mab,cb->mca', basis_vals.astype(jnp.float32), near_val.astype(jnp.float32))
    return jnp.einsum('mc,mca->ca', radial_mix, partial_value, precision=lax.Precision.HIGHEST)

def column_messages(ext_pos, ext_val, radial_mix, block_size):
    cell_count = ext_pos.shape[2] - 2

    def one_block(block_start):
        z_ids = block_start + jnp.arange(block_size, dtype=jnp.int32)
        return jax.vmap(lambda z_index: cell_messages(ext_pos, ext_val, radial_mix, z_index))(z_ids)
    starts = jnp.arange(0, cell_count, block_size, dtype=jnp.int32)
    result = lax.map(one_block, starts)
    return result.reshape(cell_count, ext_val.shape[3], ext_val.shape[4])

def wrap_pad(array):
    array = jnp.concatenate([array[-1:], array, array[:1]], axis=0)
    array = jnp.concatenate([array[:, -1:], array, array[:, :1]], axis=1)
    return jnp.pad(array, ((0, 0), (0, 0), (1, 1), (0, 0), (0, 0)))

def reference(features, positions, species, atom_mask, charge_table, k_vectors, k_weights, w_value, w_charge, w_radial, w_out):
    highest = lax.Precision.HIGHEST
    size_x, size_y, cell_count = (features.shape[0], features.shape[1], features.shape[2])
    atom_count = features.shape[4]
    chan_count = w_value.shape[2]
    kcount = k_vectors.shape[1]
    live = atom_mask.astype(jnp.float32)
    live_wide = live[:, :, :, None, :]
    onehot = (species[:, :, :, None, :] == jnp.arange(NSPEC, dtype=jnp.int32)[:, None]).astype(jnp.float32)
    offsets = jnp.einsum('sc,xyzsa->xyzca', charge_table, onehot, precision=highest)
    grid_x = jnp.broadcast_to(jnp.arange(size_x, dtype=jnp.float32)[:, None, None], (size_x, size_y, cell_count))
    grid_y = jnp.broadcast_to(jnp.arange(size_y, dtype=jnp.float32)[None, :, None], (size_x, size_y, cell_count))
    grid_z = jnp.broadcast_to(jnp.arange(cell_count, dtype=jnp.float32)[None, None, :], (size_x, size_y, cell_count))
    anchor = jnp.stack([grid_x, grid_y, grid_z], axis=-1)
    absolute = positions + anchor[..., None]
    abs_cols = absolute.reshape(size_x * size_y, cell_count, 3, atom_count)
    ewald_scale = 1.0 / math.sqrt(kcount * size_x * size_y * cell_count * atom_count)
    pos_pad = wrap_pad(positions)
    zero = jnp.zeros((), jnp.int32)

    def trig_of(column):
        phases = jnp.einsum('dk,zda->kza', k_vectors, column, precision=highest).reshape(kcount, cell_count * atom_count)
        return (jnp.cos(phases), jnp.sin(phases))
    hidden = features
    potential = jnp.zeros((size_x, size_y, cell_count, chan_count, atom_count), jnp.float32)
    for layer in range(LAYERS):
        values_all = jnp.einsum('dc,xyzda->xyzca', w_value[layer].astype(jnp.float32), hidden.astype(jnp.float32)).astype(jnp.bfloat16) * live_wide.astype(jnp.bfloat16)
        charges = (jnp.einsum('dc,xyzda->xyzca', w_charge[layer].astype(jnp.float32), hidden.astype(jnp.float32)) + offsets) * live_wide
        charge_cols = jnp.moveaxis(charges.reshape(size_x * size_y, cell_count, chan_count, atom_count), 2, 1).reshape(size_x * size_y, chan_count, cell_count * atom_count)

        def add_column(carry, inputs):
            column, charge_col = inputs
            cos_t, sin_t = trig_of(column)
            return ((carry[0] + jnp.dot(charge_col, cos_t.T, precision=highest, preferred_element_type=jnp.float32), carry[1] + jnp.dot(charge_col, sin_t.T, precision=highest, preferred_element_type=jnp.float32)), None)
        start_sums = (jnp.zeros((chan_count, kcount), jnp.float32), jnp.zeros((chan_count, kcount), jnp.float32))
        (s_cos, s_sin), _ = lax.scan(add_column, start_sums, (abs_cols, charge_cols))
        weighted_cos = s_cos * k_weights[None, :]
        weighted_sin = s_sin * k_weights[None, :]

        def column_potential(column):
            cos_t, sin_t = trig_of(column)
            total = jnp.dot(weighted_cos, cos_t, precision=highest, preferred_element_type=jnp.float32) + jnp.dot(weighted_sin, sin_t, precision=highest, preferred_element_type=jnp.float32)
            return jnp.moveaxis((total * ewald_scale).reshape(chan_count, cell_count, atom_count), 0, 1)
        potential = lax.map(column_potential, abs_cols).reshape(size_x, size_y, cell_count, chan_count, atom_count)
        val_pad = wrap_pad(values_all)

        def one_column(flat):
            index_x = (flat // size_y).astype(jnp.int32)
            index_y = (flat % size_y).astype(jnp.int32)
            ext_pos = lax.dynamic_slice(pos_pad, (index_x, index_y, zero, zero, zero), (3, 3, cell_count + 2, 3, atom_count))
            ext_val = lax.dynamic_slice(val_pad, (index_x, index_y, zero, zero, zero), (3, 3, cell_count + 2, chan_count, atom_count))
            return column_messages(ext_pos, ext_val, w_radial[layer], ZBLOCK)
        radial = lax.map(one_column, jnp.arange(size_x * size_y, dtype=jnp.int32)).reshape(size_x, size_y, cell_count, chan_count, atom_count)
        activated = jax.nn.silu(radial + potential).astype(jnp.bfloat16)
        update = jnp.einsum('cd,xyzca->xyzda', w_out[layer].astype(jnp.float32), activated.astype(jnp.float32))
        hidden = (hidden.astype(jnp.float32) + update * live_wide).astype(jnp.bfloat16)
    return (hidden, potential)
```

```python
import functools
import math

import jax
import jax.numpy as jnp
import numpy as np
from jax import lax
from jax.experimental import pallas as pl
from jax.experimental.pallas import tpu as pltpu
from jax.sharding import PartitionSpec as P

F32 = jnp.float32
BF16 = jnp.bfloat16
MESH = pl.DeviceIdType.MESH
LOG2E = math.log2(math.e)
ROWS = 32


def trig_polynomials():
    t = 0.25 * (1.0 - np.cos(np.pi * (np.arange(400) + 0.5) / 400)) + 1e-9
    u = t * t
    cos_c = np.polynomial.Polynomial.fit(u, np.cos(2 * np.pi * t), 6).convert().coef
    sin_c = np.polynomial.Polynomial.fit(u, np.sin(2 * np.pi * t) / t, 5).convert().coef
    return [float(c) for c in cos_c], [float(c) for c in sin_c]


COS_C, SIN_C = trig_polynomials()


def horner(coefs, u):
    total = coefs[-1]
    for c in coefs[-2::-1]:
        total = total * u + c
    return total


def dot(a, b):
    return jnp.dot(a, b, preferred_element_type=F32)


def kernel(
    ngx, ngy, layers,
    feat_ref, pos_ref, spec_ref, mask_ref, table_ref, kvec_ref, kw_ref, wv_ref, wc_ref, wr_ref, wo_ref,
    out_ref, pot_ref,
    inner1, inner2, edge1, edge2,
    trig, pos9, pos_a, val9, val_t, offs, live, ch_t, acc,
    s_send, rs_recv, ar_send, ar_recv, ag,
    psend, precv, vsend, vrecv, rss, rsr, ars, arr, ags, agr,
):
    gx = lax.axis_index("gx")
    gy = lax.axis_index("gy")
    cells, feat_dim, atoms = feat_ref.shape
    chans = wv_ref.shape[2]
    kcount = kvec_ref.shape[1]
    basis = wr_ref.shape[1]
    right, left = lax.rem(gx + 1, ngx), lax.rem(gx + ngx - 1, ngx)
    up, down = lax.rem(gy + 1, ngy), lax.rem(gy + ngy - 1, ngy)
    part = chans // ngx

    barrier = pltpu.get_barrier_semaphore()
    for j in range(1, ngx):
        pl.semaphore_signal(barrier, inc=1, device_id={"gx": lax.rem(gx + j, ngx)}, device_id_type=MESH)
    for j in range(1, ngy):
        pl.semaphore_signal(barrier, inc=1, device_id={"gy": lax.rem(gy + j, ngy)}, device_id_type=MESH)
    pl.semaphore_wait(barrier, ngx + ngy - 2)

    def remote(src, dst, ssem, rsem, where):
        copy = pltpu.make_async_remote_copy(
            src_ref=src, dst_ref=dst, send_sem=ssem, recv_sem=rsem, device_id=where, device_id_type=MESH
        )
        copy.start()
        return copy

    near = ((3, {"gy": up}), (5, {"gy": down}), (1, {"gx": right}), (7, {"gx": left}))

    def send_own(buf, ssem, rsem):
        return {slot: remote(buf.at[4], buf.at[slot], ssem.at[slot], rsem.at[slot], where) for slot, where in near}

    def forward(buf, ssem, rsem, copies):
        for src, to_right, to_left in ((3, 0, 6), (5, 2, 8)):
            copies[src].wait_recv()
            copies[to_right] = remote(buf.at[src], buf.at[to_right], ssem.at[to_right], rsem.at[to_right], {"gx": right})
            copies[to_left] = remote(buf.at[src], buf.at[to_left], ssem.at[to_left], rsem.at[to_left], {"gx": left})

    pos9[4] = pos_ref[...] * 8.0
    pos_copies = send_own(pos9, psend, precv)

    def project(layer, hidden_of):
        wv = wv_ref[layer].astype(F32).T.astype(BF16)
        wc = wc_ref[layer].astype(F32).T.astype(BF16)
        w = jnp.concatenate([wv, wc], axis=0)
        for z in range(cells):
            both = dot(w, hidden_of(z))
            alive = live[z : z + 1, :]
            values = both[:chans].astype(BF16).astype(F32) * alive
            val9[layer, 4, z] = values.astype(BF16)
            charge = (both[chans:] + offs[z]) * alive
            high = charge.astype(BF16).astype(F32)
            stacked = jnp.concatenate([high, charge - high], axis=0)
            ch_t[z * atoms : (z + 1) * atoms, :] = stacked.T.astype(BF16)

    def transpose_values(layer, slots):
        for slot in slots:
            def body(z, carry, slot=slot):
                rows = pl.ds(pl.multiple_of(z * atoms, atoms), atoms)
                val_t[slot, rows, :] = val9[layer, slot, z].astype(F32).T.astype(BF16)
                return carry

            lax.fori_loop(0, cells, body, 0)

    def basis_tile(store, centre, zs, dz, slot, dx, dy, row0):
        r2 = None
        for d, shift in enumerate((dx * 8.0, dy * 8.0, dz * 8.0)):
            near_row = pos9[slot, zs, d : d + 1, :] + shift
            diff = near_row - centre[d]
            r2 = diff * diff if r2 is None else r2 + diff * diff
        r2 = jnp.minimum(jnp.maximum(r2, 1e-30), 64.0)
        r = r2 * lax.rsqrt(r2)
        gap = 64.0 - r2
        envelope = gap * gap
        if dz == 0 and not isinstance(slot, jax.Array) and slot == 4:
            a = lax.broadcasted_iota(jnp.int32, r2.shape, 0) + row0
            b = lax.broadcasted_iota(jnp.int32, r2.shape, 1)
            envelope = jnp.where(a == b, 0.0, envelope)
        mid = basis // 2
        off = r - (mid + 0.5)
        step = r * (2.0 * LOG2E) - 2.0 * mid * LOG2E
        g = jnp.exp2(off * off * (-LOG2E)) * envelope
        q = jnp.exp2(step)
        store(mid, g)
        h = g
        for m in range(mid + 1, basis):
            h = h * q
            store(m, h)
        qi = jnp.exp2(-step)
        h = g
        for m in range(mid - 1, -1, -1):
            h = h * qi
            store(m, h)

    def step_at(layer, cache, z, dzs, slots):
        width = len(dzs) * atoms
        first = pl.multiple_of((z + dzs[0]) * atoms, atoms) if isinstance(z, jax.Array) else (z + dzs[0]) * atoms
        vals = jnp.concatenate([val_t[slot, pl.ds(first, width), :] for slot, _, _ in slots], axis=0)
        mid = basis // 2
        mix = [
            wr_ref[layer, m : m + 1, :] * (math.exp(-((m - mid) ** 2) - (m - mid)) / 4096.0) for m in range(basis)
        ]
        for block in range(atoms // ROWS):
            base = block * basis * ROWS
            if layer == 0 or len(dzs) < 3:
                here = pos_a[z, block * ROWS : (block + 1) * ROWS, :]
                centre = [jnp.broadcast_to(here[:, d : d + 1], (ROWS, atoms)) for d in range(3)]
                for i, (slot, dx, dy) in enumerate(slots):
                    for j, dz in enumerate(dzs):
                        col = (i * len(dzs) + j) * atoms

                        def store(m, value, col=col):
                            cache[base + m * ROWS : base + (m + 1) * ROWS, col : col + atoms] = value.astype(BF16)

                        basis_tile(store, centre, z + dz, dz, slot, dx, dy, block * ROWS)
            sums = dot(cache[base : base + basis * ROWS, :], vals)
            total = sums[:ROWS] * mix[0]
            for m in range(1, basis):
                total += sums[m * ROWS : (m + 1) * ROWS] * mix[m]
            acc[z, block * ROWS : (block + 1) * ROWS, :] += total

    def columns(layer, inner, edge, slots):
        step_at(layer, edge, 0, (0, 1), slots)

        def body(z, carry):
            step_at(layer, inner.at[z - 1], z, (-1, 0, 1), slots)
            return carry

        lax.fori_loop(1, cells - 1, body, 0)
        step_at(layer, edge, cells - 1, (-1, 0), slots)

    def column_pairs(layer, straight):
        def body(i, carry):
            if straight:
                one = 1 + 2 * i
            else:
                one = 2 * i
            slots = []
            for slot in (one, 8 - one):
                dx = (slot // 3 - 1).astype(F32)
                dy = (lax.rem(slot, 3) - 1).astype(F32)
                slots.append((slot, dx, dy))
            which = i if straight else i + 2
            columns(layer, inner2.at[which], edge2, slots)
            return carry

        lax.fori_loop(0, 2, body, 0)

    live[...] = mask_ref[...].astype(F32)
    table_t = table_ref[...].T
    for z in range(cells):
        kind = spec_ref[z : z + 1, :]
        total = jnp.zeros((chans, atoms), F32)
        for s in range(table_ref.shape[0]):
            total = jnp.where(kind == s, table_t[:, s : s + 1], total)
        offs[z] = total

    scale = 1.0 / math.sqrt(kcount * ngx * ngy * cells * atoms)
    kw = kw_ref[...]
    kw = jnp.concatenate([kw, kw], axis=1) * scale
    held = {}
    for layer in range(layers):
        source = feat_ref if layer == 0 else out_ref
        project(layer, lambda z: source[z])
        copies = send_own(val9.at[layer], vsend.at[layer], vrecv.at[layer])
        acc[...] = jnp.zeros_like(acc)
        if layer == 0:
            forward(pos9, psend, precv, pos_copies)
            fx, fy = gx.astype(F32), gy.astype(F32)
            kv = kvec_ref[...] * (1.0 / (2.0 * math.pi))
            kv = jnp.concatenate([kv, jnp.zeros((5, kcount), F32)], axis=0).T
            for kc in range(kcount // ROWS):
                cols = [jnp.broadcast_to(kv[kc * ROWS : (kc + 1) * ROWS, d : d + 1], (ROWS, atoms)) for d in range(3)]
                for z in range(cells):
                    t = cols[0] * (pos_ref[z, 0:1, :] + fx)
                    t += cols[1] * (pos_ref[z, 1:2, :] + fy)
                    t += cols[2] * (pos_ref[z, 2:3, :] + float(z))
                    t = t - jnp.round(t)
                    u = t * t
                    lanes = slice(z * atoms, (z + 1) * atoms)
                    trig[kc * ROWS : (kc + 1) * ROWS, lanes] = horner(COS_C, u).astype(BF16)
                    trig[kcount + kc * ROWS : kcount + (kc + 1) * ROWS, lanes] = (horner(SIN_C, u) * t).astype(BF16)
        s_both = dot(trig[...], ch_t[...]).T
        s_own = s_both[:chans] + s_both[chans:]
        for i in range(ngx):
            s_send[layer, i] = s_own[i * part : (i + 1) * part]
        rs = []
        for j in range(1, ngx):
            to = lax.rem(gx + j, ngx)
            rs.append(remote(s_send.at[layer, to], rs_recv.at[layer, j - 1], rss.at[layer, j - 1], rsr.at[layer, j - 1], {"gx": to}))
        forward(val9.at[layer], vsend.at[layer], vrecv.at[layer], copies)
        if layer == 0:
            for z in range(cells):
                pos_a[z] = jnp.concatenate([pos9[4, z], jnp.zeros((5, atoms), F32)], axis=0).T
        transpose_values(layer, (4, 3, 5))
        columns(layer, inner1, edge1, [(4, 0.0, 0.0)])
        total = s_send[layer, gx]
        for j, copy in enumerate(rs):
            copy.wait_recv()
            total += rs_recv[layer, j]
        ar_send[layer] = total
        ar = []
        for j in range(1, ngy):
            to = lax.rem(gy + j, ngy)
            ar.append(remote(ar_send.at[layer], ar_recv.at[layer, j - 1], ars.at[layer, j - 1], arr.at[layer, j - 1], {"gy": to}))
        for slot in (1, 7):
            copies[slot].wait_recv()
            if layer == 0:
                pos_copies[slot].wait_recv()
        transpose_values(layer, (1, 7))
        column_pairs(layer, True)
        total = ar_send[layer]
        for j, copy in enumerate(ar):
            copy.wait_recv()
            total += ar_recv[layer, j]
        ag[layer, gx] = total
        gather = []
        for j in range(1, ngx):
            to = lax.rem(gx + j, ngx)
            gather.append(remote(ag.at[layer, gx], ag.at[layer, gx], ags.at[layer, j - 1], agr.at[layer, j - 1], {"gx": to}))
        for slot in (0, 2, 6, 8):
            copies[slot].wait_recv()
            if layer == 0:
                pos_copies[slot].wait_recv()
        transpose_values(layer, (0, 2, 6, 8))
        column_pairs(layer, False)
        for copy in gather:
            copy.wait_recv()
        s_all = jnp.concatenate([ag[layer, i] for i in range(ngx)], axis=0) * kw
        high = s_all.astype(BF16)
        low = (s_all - high.astype(F32)).astype(BF16)
        both = dot(jnp.concatenate([high, low], axis=0), trig[...])
        potential = both[:chans] + both[chans:]
        wo = wo_ref[layer].astype(F32).T.astype(BF16)
        for z in range(cells):
            pot = potential[:, z * atoms : (z + 1) * atoms]
            if layer == layers - 1:
                pot_ref[z] = pot
            x = acc[z].T + pot
            activated = (x / (1.0 + jnp.exp(-x))).astype(BF16)
            update = dot(wo, activated)
            out_ref[z] = (source[z].astype(F32) + update * live[z : z + 1, :]).astype(BF16)
        held[layer] = list(copies.values()) + rs + ar + gather
    for copy in pos_copies.values():
        copy.wait_send()
    for group in held.values():
        for copy in group:
            copy.wait_send()


def on_device(
    features, positions, species, atom_mask, charge_table, k_vectors, k_weights, w_value, w_charge, w_radial, w_out
):
    ngx, ngy = lax.axis_size("gx"), lax.axis_size("gy")
    cells, feat_dim, atoms = features.shape[2:]
    layers, _, chans = w_value.shape
    kcount = k_vectors.shape[1]
    basis = w_radial.shape[1]
    part = chans // ngx
    vmem = pl.BlockSpec(memory_space=pltpu.VMEM)
    dma = pltpu.SemaphoreType.DMA
    tall = basis * atoms
    hidden, potential = pl.pallas_call(
        functools.partial(kernel, ngx, ngy, layers),
        out_shape=(
            jax.ShapeDtypeStruct((cells, feat_dim, atoms), BF16),
            jax.ShapeDtypeStruct((cells, chans, atoms), F32),
        ),
        in_specs=[vmem] * 11,
        out_specs=(vmem, vmem),
        scratch_shapes=[
            pltpu.VMEM((cells - 2, tall, 3 * atoms), BF16),
            pltpu.VMEM((4, cells - 2, tall, 6 * atoms), BF16),
            pltpu.VMEM((tall, 2 * atoms), BF16),
            pltpu.VMEM((tall, 4 * atoms), BF16),
            pltpu.VMEM((2 * kcount, cells * atoms), BF16),
            pltpu.VMEM((9, cells, 3, atoms), F32),
            pltpu.VMEM((cells, atoms, 8), F32),
            pltpu.VMEM((layers, 9, cells, chans, atoms), BF16),
            pltpu.VMEM((9, cells * atoms, chans), BF16),
            pltpu.VMEM((cells, chans, atoms), F32),
            pltpu.VMEM((cells, atoms), F32),
            pltpu.VMEM((cells * atoms, 2 * chans), BF16),
            pltpu.VMEM((cells, atoms, chans), F32),
            pltpu.VMEM((layers, ngx, part, 2 * kcount), F32),
            pltpu.VMEM((layers, ngx - 1, part, 2 * kcount), F32),
            pltpu.VMEM((layers, part, 2 * kcount), F32),
            pltpu.VMEM((layers, ngy - 1, part, 2 * kcount), F32),
            pltpu.VMEM((layers, ngx, part, 2 * kcount), F32),
            dma((9,)), dma((9,)), dma((layers, 9)), dma((layers, 9)),
            dma((layers, ngx - 1)), dma((layers, ngx - 1)),
            dma((layers, ngy - 1)), dma((layers, ngy - 1)),
            dma((layers, ngx - 1)), dma((layers, ngx - 1)),
        ],
        compiler_params=pltpu.CompilerParams(
            collective_id=0, has_side_effects=True, vmem_limit_bytes=56 * 2**20
        ),
    )(
        features[0, 0], positions[0, 0], species[0, 0], atom_mask[0, 0], charge_table, k_vectors,
        k_weights[None, :], w_value, w_charge, w_radial, w_out,
    )
    return hidden[None, None], potential[None, None]


def solution(mesh):
    cell = ("gx", "gy", None, None)
    in_specs = (P(*cell, None), P(*cell, None), P(*cell), P(*cell)) + (P(),) * 7
    out_specs = (P(*cell, None), P(*cell, None))
    return jax.shard_map(on_device, mesh=mesh, in_specs=in_specs, out_specs=out_specs, check_vma=False)
```
